32 devices in a mesh: seq: 8 (over z, y), head: 4 (over x, core).
Axes of the slice: x: 2, y: 2, z: 4, core: 2. Of those that a mesh axis runs over, the one named last changes fastest.
Arguments:
- queries: bfloat16 [4096, 4096], P(('seq', 'head')), may hold values from -100 to 100
- keys_in: bfloat16 [4096, 4096], P(('seq', 'head')), may hold values from -16 to 16
- values_in: bfloat16 [4096, 4096], P(('seq', 'head')), may hold values from -16 to 16
- grad_out: bfloat16 [4096, 4096], P(('seq', 'head')), may hold values from -6 to 6
Outputs:
- attended: bfloat16 [4096, 4096], P(('seq', 'head'))
- grad_queries: bfloat16 [4096, 4096], P(('seq', 'head'))
- grad_keys: bfloat16 [4096, 4096], P(('seq', 'head'))
- grad_values: bfloat16 [4096, 4096], P(('seq', 'head'))
The draws below stay inside these ranges and needn't reach their ends.
All inputs are finite; a program needn't handle non-finite values.
Results may differ from the reference program's by a relative error of at most 0.0052.
Values may be sent and summed in bfloat16 or wider, within the bound.
No kernel may reach another device: no remote copies, remote signals or barrier semaphores. Data moves between devices by JAX's collectives and lax.ppermute only.
A program may use at most 64 MiB of HBM per device.

```python
import jax
import jax.numpy as jnp
from jax import lax

HEADS = 32
HD = 128
SHARD = 512
CROWS = 16
TOKENS = 4096
N_SEQ = 8


def drifting(key, salt):
    rough = jax.random.normal(jax.random.fold_in(key, salt), (TOKENS, HEADS * HD), jnp.float32)
    slow = jax.random.normal(jax.random.fold_in(key, salt + 1), (TOKENS // 64, 1, HEADS * HD), jnp.float32)
    slow = jnp.broadcast_to(slow, (TOKENS // 64, 64, HEADS * HD)).reshape(TOKENS, HEADS * HD)
    return jnp.clip(rough + slow, -15.0, 15.0)


def draw_keys_in(key, part):
    return drifting(key, 11).astype(jnp.bfloat16)


def draw_values_in(key, part):
    return drifting(key, 31).astype(jnp.bfloat16)


def draw_queries(key, part):
    drawn = jax.random.normal(jax.random.fold_in(key, 51), (TOKENS, HEADS * HD), jnp.float32)
    drawn = jnp.clip(drawn, -6.0, 6.0)
    return drawn.astype(jnp.bfloat16)


def levels(stream_key, extent, shards, least, high):
    gain = 1.0
    for dim, parts in shards:
        draws = jax.random.uniform(jax.random.fold_in(jax.random.fold_in(stream_key, 6), dim), (parts,), jnp.float32, least / len(shards), high / len(shards))
        gain = gain * jnp.repeat(jnp.exp(draws), extent[dim] // parts).reshape((-1,) + (1,) * (len(extent) - 1 - dim))
    return gain


def scatter_about(rng, shape, spread, reach, shards=(), kind=jnp.bfloat16):
    entries = jax.random.normal(rng, shape, jnp.float32) * spread
    if len(shards) > 0:
        entries = levels(rng, shape, shards, -0.22, 0.18) * entries
    return jnp.clip(entries, min=-reach, max=reach).astype(kind)


def setup_inputs(seed: int = 0) -> dict:
    keys = jax.random.split(jax.random.key(seed), 5)
    queries = draw_queries(jax.random.fold_in(keys[4], 71), 0)
    keys_in = draw_keys_in(jax.random.fold_in(keys[4], 71), 0)
    values_in = draw_values_in(jax.random.fold_in(keys[4], 71), 0)
    grad_out = scatter_about(keys[3], (TOKENS, HEADS * HD), 1.0, 6.0, ((0, 32),))
    return dict(queries=queries, keys_in=keys_in, values_in=values_in, grad_out=grad_out)


def reference(queries, keys_in, values_in, grad_out):
    depth = N_SEQ.bit_length() - 1
    scale_q = HD ** -0.5
    pool_size = SHARD // CROWS
    q_all = queries.reshape(N_SEQ, SHARD, HEADS, HD)
    k_all = keys_in.reshape(N_SEQ, SHARD, HEADS, HD)
    v_all = values_in.reshape(N_SEQ, SHARD, HEADS, HD)
    g_all = grad_out.reshape(N_SEQ, SHARD, HEADS, HD)
    pooled_k = jnp.mean(k_all.astype(jnp.float32).reshape(N_SEQ, CROWS, pool_size, HEADS, HD), axis=2).transpose(0, 2, 1, 3)
    pooled_v = jnp.mean(v_all.astype(jnp.float32).reshape(N_SEQ, CROWS, pool_size, HEADS, HD), axis=2).transpose(0, 2, 1, 3)
    group_k = []
    group_v = []
    for level in range(depth):
        width_here = 2 ** level
        group_k.append(jnp.mean(pooled_k.reshape(N_SEQ // width_here, width_here, HEADS, CROWS, HD), axis=1))
        group_v.append(jnp.mean(pooled_v.reshape(N_SEQ // width_here, width_here, HEADS, CROWS, HD), axis=1))
    log_counts = jnp.repeat(jnp.log(float(pool_size) * 2.0 ** jnp.arange(depth, dtype=jnp.float32)), CROWS)
    offsets = jnp.concatenate([jnp.zeros((SHARD,), jnp.float32), log_counts.astype(jnp.float32)])

    def per_device(device):
        sib_k = jnp.stack([group_k[level][(device >> level) ^ 1] for level in range(depth)], axis=1)
        sib_v = jnp.stack([group_v[level][(device >> level) ^ 1] for level in range(depth)], axis=1)
        sib_k = lax.optimization_barrier(sib_k.reshape(HEADS, depth * CROWS, HD).astype(jnp.bfloat16)).astype(jnp.float32)
        sib_v = lax.optimization_barrier(sib_v.reshape(HEADS, depth * CROWS, HD).astype(jnp.bfloat16)).astype(jnp.float32)
        query_here = q_all[device].astype(jnp.float32)
        grad_here = g_all[device].astype(jnp.float32)
        keys_full = jnp.concatenate([k_all[device].astype(jnp.float32).transpose(1, 0, 2), sib_k], axis=1)
        values_full = jnp.concatenate([v_all[device].astype(jnp.float32).transpose(1, 0, 2), sib_v], axis=1)
        scores = jnp.einsum("shd,htd->hst", query_here, keys_full) * scale_q + offsets
        probs = jax.nn.softmax(scores, axis=-1)
        probs_low = lax.optimization_barrier(probs.astype(jnp.bfloat16)).astype(jnp.float32)
        attended = jnp.einsum("hst,htd->shd", probs_low, values_full).astype(jnp.bfloat16)
        dprob = jnp.einsum("shd,htd->hst", grad_here, values_full)
        dscore = scale_q * probs * (dprob - jnp.sum(probs * dprob, axis=-1, keepdims=True))
        dscore_low = lax.optimization_barrier(dscore.astype(jnp.bfloat16)).astype(jnp.float32)
        grad_query = jnp.einsum("hst,htd->shd", dscore_low, keys_full).astype(jnp.bfloat16)
        dkeys = jnp.einsum("hst,shd->htd", dscore_low, query_here)
        dvalues = jnp.einsum("hst,shd->htd", probs_low, grad_here)
        return (attended, grad_query, dkeys[:, :SHARD], dvalues[:, :SHARD],
                dkeys[:, SHARD:].reshape(HEADS, depth, CROWS, HD), dvalues[:, SHARD:].reshape(HEADS, depth, CROWS, HD))

    results = lax.map(per_device, jnp.arange(N_SEQ, dtype=jnp.int32))
    grad_pool_k = jnp.zeros((N_SEQ, HEADS, CROWS, HD), jnp.float32)
    grad_pool_v = jnp.zeros((N_SEQ, HEADS, CROWS, HD), jnp.float32)
    device_ids = jnp.arange(N_SEQ, dtype=jnp.int32)
    for level in range(depth):
        width_here = 2 ** level
        sums_k = jnp.sum(results[4][:, :, level].reshape(N_SEQ // width_here, width_here, HEADS, CROWS, HD), axis=1)
        sums_v = jnp.sum(results[5][:, :, level].reshape(N_SEQ // width_here, width_here, HEADS, CROWS, HD), axis=1)
        grad_pool_k = grad_pool_k + sums_k[(device_ids >> level) ^ 1] / float(width_here)
        grad_pool_v = grad_pool_v + sums_v[(device_ids >> level) ^ 1] / float(width_here)
    grad_k = results[2] + jnp.repeat(grad_pool_k / float(pool_size), pool_size, axis=2)
    grad_v = results[3] + jnp.repeat(grad_pool_v / float(pool_size), pool_size, axis=2)
    attended = results[0].reshape(TOKENS, HEADS * HD)
    grad_q = results[1].reshape(TOKENS, HEADS * HD)
    grad_k = grad_k.transpose(0, 2, 1, 3).reshape(TOKENS, HEADS * HD).astype(jnp.bfloat16)
    grad_v = grad_v.transpose(0, 2, 1, 3).reshape(TOKENS, HEADS * HD).astype(jnp.bfloat16)
    return (attended, grad_q, grad_k, grad_v)
```

```python
import functools
import math

import jax
import jax.numpy as jnp
from jax import lax
from jax.experimental import pallas as pl
from jax.experimental.pallas import tpu as pltpu
from jax.sharding import PartitionSpec as P

HD = 128
CROWS = 16
SCALE = HD**-0.5


def swapped(block, axis, mask):
    count = lax.axis_size(axis)
    return lax.ppermute(block, axis, [(i, i ^ mask) for i in range(count)])


def attention_kernel(parts, depth, pool_size, *refs):
    blocks = refs[:parts]
    coarse_ref = refs[parts]
    out_refs = refs[parts + 1 : 2 * parts + 1]
    local_ref, coarse_grad_ref = refs[2 * parts + 1 :]
    rows = blocks[0].shape[1]
    own = parts * rows

    def whole(which):
        return jnp.concatenate([b[which] for b in blocks], axis=0)

    keys = jnp.concatenate([whole(0), coarse_ref[0]], axis=0)
    values = jnp.concatenate([whole(1), coarse_ref[1]], axis=0)
    queries, grads = whole(2), whole(3)
    seen = keys.shape[0]

    def dot(a, b, over):
        return lax.dot_general(
            a, b, (((over[0],), (over[1],)), ((), ())), preferred_element_type=jnp.float32
        )

    scores = dot(keys, queries, (1, 1)) * (SCALE * math.log2(math.e))
    row = lax.broadcasted_iota(jnp.int32, (seen - own, 1), 0)
    offset = (row // CROWS).astype(jnp.float32) + math.log2(pool_size)
    scores = jnp.concatenate([scores[:own], scores[own:] + offset], axis=0)
    powers = jnp.exp2(scores - jnp.max(scores, axis=0, keepdims=True))
    probs = powers * (1.0 / jnp.sum(powers, axis=0, keepdims=True))
    probs_low = probs.astype(jnp.bfloat16)
    dprob = dot(values, grads, (1, 1))
    mean = jnp.sum(probs * dprob, axis=0, keepdims=True)
    dscore = (probs * SCALE * (dprob - mean)).astype(jnp.bfloat16)
    attended = dot(values, probs_low, (0, 0)).T.astype(jnp.bfloat16)
    grad_query = dot(keys, dscore, (0, 0)).T.astype(jnp.bfloat16)
    dkeys = dot(dscore, queries, (1, 0))
    dvalues = dot(probs_low, grads, (1, 0))
    for part in range(parts):
        here = slice(part * rows, (part + 1) * rows)
        out_refs[part][0] = attended[here]
        out_refs[part][1] = grad_query[here]
    local_ref[0] = dkeys[:own]
    local_ref[1] = dvalues[:own]
    coarse_grad_ref[0] = dkeys[own:]
    coarse_grad_ref[1] = dvalues[own:]


def attention(blocks, coarse, first_head, depth, pool_size):
    parts = len(blocks)
    _, rows, width = blocks[0].shape
    heads = width // HD
    own = parts * rows
    extra = coarse.shape[1]
    seen = own + extra
    by_head = lambda h: (0, 0, h)
    outs = pl.pallas_call(
        functools.partial(attention_kernel, parts, depth, pool_size),
        grid=(heads,),
        in_specs=[pl.BlockSpec((4, rows, HD), by_head)] * parts
        + [pl.BlockSpec((2, extra, HD), lambda h: (0, 0, first_head + h))],
        out_specs=[pl.BlockSpec((2, rows, HD), by_head)] * parts
        + [pl.BlockSpec((2, own, HD), by_head), pl.BlockSpec((2, extra, HD), by_head)],
        out_shape=[jax.ShapeDtypeStruct((2, rows, width), jnp.bfloat16)] * parts
        + [
            jax.ShapeDtypeStruct((2, own, width), jnp.float32),
            jax.ShapeDtypeStruct((2, extra, width), jnp.float32),
        ],
        compiler_params=pltpu.CompilerParams(vmem_limit_bytes=40 * 1024 * 1024),
        cost_estimate=pl.CostEstimate(
            flops=12 * heads * own * seen * HD,
            bytes_accessed=24 * own * width,
            transcendentals=heads * own * seen,
        ),
        name="attention",
    )(*blocks, coarse)
    return outs[:parts], outs[parts], outs[parts + 1]


def on_device(queries, keys_in, values_in, grad_out):
    seq_count = lax.axis_size("seq")
    parts = lax.axis_size("head")
    me = lax.axis_index("head")
    depth = seq_count.bit_length() - 1
    rows, columns = queries.shape
    own = rows * parts
    pool_size = own // CROWS
    width = columns // parts
    heads = width // HD
    groups = 2 if heads % 2 == 0 else 1
    span = width // groups
    arrays = (keys_in, values_in, queries, grad_out)

    def pooled(x):
        return jnp.mean(x.astype(jnp.float32).reshape(rows // pool_size, pool_size, columns), axis=1)

    pooled_here = jnp.stack([pooled(keys_in), pooled(values_in)], axis=0)

    def column(part, group=0):
        return (me ^ part) * width + group * span

    pooled_parts = []
    for part in range(parts):
        block = lax.dynamic_slice_in_dim(pooled_here, column(part), width, axis=2)
        pooled_parts.append(swapped(block, "head", part) if part else block)
    mean_now = jnp.concatenate(pooled_parts, axis=1)

    blocks = []
    for group in range(groups):
        here = []
        for part in range(parts):
            block = jnp.stack(
                [lax.dynamic_slice_in_dim(x, column(part, group), span, axis=1) for x in arrays]
            )
            here.append(swapped(block, "head", part) if part else block)
        blocks.append(here)

    siblings = []
    for level in range(depth):
        received = swapped(mean_now, "seq", 1 << level)
        siblings.append(received)
        mean_now = 0.5 * (mean_now + received)
    coarse = jnp.concatenate(siblings, axis=1).astype(jnp.bfloat16)

    outs = [jnp.zeros((rows, columns), jnp.bfloat16) for _ in range(4)]
    for group in range(groups):
        sent, local, coarse_grad = attention(
            blocks[group], coarse, group * (heads // groups), depth, pool_size
        )
        coarse_grad = coarse_grad.reshape(2, depth, CROWS, span)
        for part in range(parts):
            back = swapped(sent[part], "head", part) if part else sent[part]
            for which in range(2):
                outs[which] = lax.dynamic_update_slice(
                    outs[which], back[which], (0, column(part, group))
                )
        above = jnp.zeros((2, CROWS, span), jnp.float32)
        for level in reversed(range(depth)):
            outgoing = coarse_grad[:, level] + 0.5 * above
            above = 0.5 * above + swapped(outgoing, "seq", 1 << level)
        above = above / float(pool_size)
        per = rows // pool_size
        for part in range(parts):
            spread = jnp.repeat(above[:, part * per : (part + 1) * per], pool_size, axis=1)
            total = (local[:, part * rows : (part + 1) * rows] + spread).astype(jnp.bfloat16)
            back = swapped(total, "head", part) if part else total
            for which in range(2):
                outs[2 + which] = lax.dynamic_update_slice(
                    outs[2 + which], back[which], (0, column(part, group))
                )
    return tuple(outs)


def solution(mesh):
    placed = (P(("seq", "head"), None),) * 4
    return jax.shard_map(
        on_device, mesh=mesh, in_specs=placed, out_specs=placed, check_vma=False
    )
```

```python
import functools
import math

import jax
import jax.numpy as jnp
from jax import lax
from jax.experimental import pallas as pl
from jax.experimental.pallas import tpu as pltpu
from jax.sharding import PartitionSpec as P

HD = 128
CROWS = 16
SCALE = HD**-0.5


def swapped(block, axis, mask):
    count = lax.axis_size(axis)
    return lax.ppermute(block, axis, [(i, i ^ mask) for i in range(count)])


def attention_kernel(parts, depth, pool_size, *refs):
    blocks = refs[:parts]
    coarse_ref = refs[parts]
    out_refs = refs[parts + 1 : 2 * parts + 1]
    local_ref, coarse_grad_ref = refs[2 * parts + 1 :]
    rows = blocks[0].shape[1]
    own = parts * rows

    def whole(which):
        return jnp.concatenate([b[which] for b in blocks], axis=0)

    keys = jnp.concatenate([whole(0), coarse_ref[0]], axis=0)
    values = jnp.concatenate([whole(1), coarse_ref[1]], axis=0)
    queries, grads = whole(2), whole(3)
    seen = keys.shape[0]

    def dot(a, b, over):
        return lax.dot_general(
            a, b, (((over[0],), (over[1],)), ((), ())), preferred_element_type=jnp.float32
        )

    scores = dot(keys, queries, (1, 1)) * (SCALE * math.log2(math.e))
    row = lax.broadcasted_iota(jnp.int32, (seen - own, 1), 0)
    offset = (row // CROWS).astype(jnp.float32) + math.log2(pool_size)
    scores = jnp.concatenate([scores[:own], scores[own:] + offset], axis=0)
    powers = jnp.exp2(scores - jnp.max(scores, axis=0, keepdims=True))
    probs = powers * (1.0 / jnp.sum(powers, axis=0, keepdims=True))
    probs_low = probs.astype(jnp.bfloat16)
    dprob = dot(values, grads, (1, 1))
    mean = jnp.sum(probs * dprob, axis=0, keepdims=True)
    dscore = (probs * SCALE * (dprob - mean)).astype(jnp.bfloat16)
    attended = dot(values, probs_low, (0, 0)).T.astype(jnp.bfloat16)
    grad_query = dot(keys, dscore, (0, 0)).T.astype(jnp.bfloat16)
    dkeys = dot(dscore, queries, (1, 0))
    dvalues = dot(probs_low, grads, (1, 0))
    for part in range(parts):
        here = slice(part * rows, (part + 1) * rows)
        out_refs[part][0] = attended[here]
        out_refs[part][1] = grad_query[here]
    local_ref[0] = dkeys[:own]
    local_ref[1] = dvalues[:own]
    coarse_grad_ref[0] = dkeys[own:]
    coarse_grad_ref[1] = dvalues[own:]


def attention(blocks, coarse, first, heads, depth, pool_size):
    parts = len(blocks)
    rows = blocks[0].shape[1]
    width = heads * HD
    own = parts * rows
    extra = coarse.shape[1]
    seen = own + extra

    def block_spec(lead, height, total):
        skip = first if total > width else 0
        return pl.BlockSpec((lead, height, HD), lambda h: (0, 0, skip + h))

    outs = pl.pallas_call(
        functools.partial(attention_kernel, parts, depth, pool_size),
        grid=(heads,),
        in_specs=[block_spec(4, rows, b.shape[2]) for b in blocks]
        + [block_spec(2, extra, coarse.shape[2])],
        out_specs=[block_spec(2, rows, width)] * parts
        + [block_spec(2, own, width), block_spec(2, extra, width)],
        out_shape=[jax.ShapeDtypeStruct((2, rows, width), jnp.bfloat16)] * parts
        + [
            jax.ShapeDtypeStruct((2, own, width), jnp.float32),
            jax.ShapeDtypeStruct((2, extra, width), jnp.float32),
        ],
        compiler_params=pltpu.CompilerParams(vmem_limit_bytes=40 * 1024 * 1024),
        cost_estimate=pl.CostEstimate(
            flops=12 * heads * own * seen * HD,
            bytes_accessed=24 * own * width,
            transcendentals=heads * own * seen,
        ),
        name="attention",
    )(*blocks, coarse)
    return outs[:parts], outs[parts], outs[parts + 1]


def on_device(queries, keys_in, values_in, grad_out):
    seq_count = lax.axis_size("seq")
    parts = lax.axis_size("head")
    me = lax.axis_index("head")
    depth = seq_count.bit_length() - 1
    rows, columns = queries.shape
    own = rows * parts
    pool_size = own // CROWS
    per = rows // pool_size
    width = columns // parts
    heads = width // HD
    split = [heads - heads // 2, heads // 2][: min(heads, 2)]
    groups = len(split)
    starts = [sum(split[:g]) for g in range(groups)]
    far = range(2, parts)
    arrays = (keys_in, values_in, queries, grad_out)

    def column(part, head=0):
        return (me ^ part) * width + head * HD

    def slab(part, head, size):
        return jnp.stack(
            [lax.dynamic_slice_in_dim(x, column(part, head), size, axis=1) for x in arrays]
        )

    landed = {}

    def send(block, part, name):
        landed[name] = swapped(block, "head", part)

    def after(block, names):
        for name in names:
            if name in landed:
                block, landed[name] = lax.optimization_barrier((block, landed[name]))
        return block

    slabs = [[slab(part, starts[g], split[g] * HD) for part in far] for g in range(groups)]
    *slabs[0], keys_now, values_now = lax.optimization_barrier((*slabs[0], keys_in, values_in))
    pooled_here = jnp.stack(
        [
            jnp.mean(x.astype(jnp.float32).reshape(per, pool_size, columns), axis=1)
            for x in (keys_now, values_now)
        ]
    )
    pooled_parts = []
    for part in range(parts):
        block = lax.dynamic_slice_in_dim(pooled_here, column(part), width, axis=2)
        pooled_parts.append(swapped(block, "head", part) if part else block)
    mean_now = jnp.concatenate(pooled_parts, axis=1)
    siblings = []
    for level in range(depth):
        received = swapped(mean_now, "seq", 1 << level)
        siblings.append(received)
        mean_now = 0.5 * (mean_now + received)

    blocks = []
    for g in range(groups):
        if g:
            at = min(1, depth - 1)
            *slabs[g], siblings[at] = lax.optimization_barrier((*slabs[g], siblings[at]))
        for part in far:
            send(slabs[g][part - 2], part, ("in", g, part))
        size = split[g] * HD
        blocks.append([slab(0, starts[g], size), swapped(slab(1, starts[g], size), "head", 1)])
    coarse = jnp.concatenate(siblings, axis=1).astype(jnp.bfloat16)

    kept, grads, sums = [], [], []
    for g in range(groups):
        here = blocks[g] + [landed["in", g, part] for part in far]
        sent, local, coarse_grad = attention(here, coarse, starts[g], split[g], depth, pool_size)
        kept.append(sent)
        grads.append(local)
        sums.append(coarse_grad)
    for g in range(groups):
        for part in far:
            send(kept[g][part], part, ("mid", g, part))
    coarse_grad = jnp.concatenate(sums, axis=2).reshape(2, depth, CROWS, width)
    order = [("mid", g, part) for g in range(groups) for part in (2, 3)]
    pace = [[name] for name in order] + [[]] * depth
    coarse_grad = after(coarse_grad, pace[0])
    above = jnp.zeros((2, CROWS, width), jnp.float32)
    for level in reversed(range(depth)):
        outgoing = coarse_grad[:, level] + 0.5 * above
        received = swapped(outgoing.astype(jnp.bfloat16), "seq", 1 << level)
        received = after(received, pace[depth - level])
        above = 0.5 * above + received.astype(jnp.float32)
    above = above / float(pool_size)

    def total(part):
        spread = jnp.repeat(above[:, part * per : (part + 1) * per], pool_size, axis=1)
        local = jnp.concatenate([g[:, part * rows : (part + 1) * rows] for g in grads], axis=2)
        return (local + spread).astype(jnp.bfloat16)

    near = [swapped(kept[g][1], "head", 1) for g in range(groups)]
    last = [total(part) for part in far]
    near_last = swapped(total(1), "head", 1)
    for part in far:
        send(last[part - 2], part, ("last", 0, part))

    outs = [jnp.zeros((rows, columns), jnp.bfloat16) for _ in range(4)]

    def place(first, back, part, head=0):
        for which in range(back.shape[0]):
            outs[first + which] = lax.dynamic_update_slice(
                outs[first + which], back[which], (0, column(part, head))
            )

    for g in range(groups):
        place(0, kept[g][0], 0, starts[g])
        place(0, near[g], 1, starts[g])
        for part in far:
            place(0, landed["mid", g, part], part, starts[g])
    place(2, total(0), 0)
    place(2, near_last, 1)
    for part in far:
        place(2, landed["last", 0, part], part)
    return tuple(outs)


def solution(mesh):
    placed = (P(("seq", "head"), None),) * 4
    return jax.shard_map(
        on_device, mesh=mesh, in_specs=placed, out_specs=placed, check_vma=False
    )
```

```python
import functools
import math

import jax
import jax.numpy as jnp
from jax import lax
from jax.experimental import pallas as pl
from jax.experimental.pallas import tpu as pltpu
from jax.sharding import PartitionSpec as P

HD = 128
CROWS = 16
SCALE = HD**-0.5
FIRST = 1
IN_GATE = 2
PACE0 = ((), (), (), ())
PACE1 = ((("mid", 0, 2),), (("mid", 0, 3),), (("last", 0, 2),), (("last", 0, 3),))
F_PACE = ((("in", 0, 2, 0),), (), (("near", 1),))


def swapped(block, axis, mask):
    count = lax.axis_size(axis)
    return lax.ppermute(block, axis, [(i, i ^ mask) for i in range(count)])


def attention_kernel(layout, depth, pool_size, *refs):
    parts, count = len(layout), sum(layout)
    blocks = []
    for pieces in layout:
        at = sum(len(b) for b in blocks)
        blocks.append(refs[at : at + pieces])
    coarse_ref = refs[count]
    out_refs = refs[count + 1 : count + 1 + parts]
    local_ref, coarse_grad_ref = refs[count + 1 + parts :]
    rows = refs[0].shape[1]
    own = parts * rows

    def whole(which):
        taken = []
        for pieces in blocks:
            each = 4 // len(pieces)
            taken.append(pieces[which // each][which % each])
        return jnp.concatenate(taken, axis=0)

    keys = jnp.concatenate([whole(0), coarse_ref[0]], axis=0)
    values = jnp.concatenate([whole(1), coarse_ref[1]], axis=0)
    queries, grads = whole(2), whole(3)
    seen = keys.shape[0]

    def dot(a, b, over):
        return lax.dot_general(
            a, b, (((over[0],), (over[1],)), ((), ())), preferred_element_type=jnp.float32
        )

    scores = dot(keys, queries, (1, 1)) * (SCALE * math.log2(math.e))
    row = lax.broadcasted_iota(jnp.int32, (seen - own, 1), 0)
    offset = (row // CROWS).astype(jnp.float32) + math.log2(pool_size)
    scores = jnp.concatenate([scores[:own], scores[own:] + offset], axis=0)
    powers = jnp.exp2(scores - jnp.max(scores, axis=0, keepdims=True))
    probs = powers * (1.0 / jnp.sum(powers, axis=0, keepdims=True))
    probs_low = probs.astype(jnp.bfloat16)
    dprob = dot(values, grads, (1, 1))
    mean = jnp.sum(probs * dprob, axis=0, keepdims=True)
    dscore = (probs * SCALE * (dprob - mean)).astype(jnp.bfloat16)
    attended = dot(values, probs_low, (0, 0)).T.astype(jnp.bfloat16)
    grad_query = dot(keys, dscore, (0, 0)).T.astype(jnp.bfloat16)
    dkeys = dot(dscore, queries, (1, 0))
    dvalues = dot(probs_low, grads, (1, 0))
    for part in range(parts):
        here = slice(part * rows, (part + 1) * rows)
        out_refs[part][0] = attended[here]
        out_refs[part][1] = grad_query[here]
    local_ref[0] = dkeys[:own]
    local_ref[1] = dvalues[:own]
    coarse_grad_ref[0] = dkeys[own:]
    coarse_grad_ref[1] = dvalues[own:]


def attention(blocks, coarse, first, heads, depth, pool_size):
    parts = len(blocks)
    layout = tuple(len(pieces) for pieces in blocks)
    flat = [piece for pieces in blocks for piece in pieces]
    rows = flat[0].shape[1]
    width = heads * HD
    own = parts * rows
    extra = coarse.shape[1]
    seen = own + extra

    def block_spec(lead, height, total):
        skip = first if total > width else 0
        return pl.BlockSpec((lead, height, HD), lambda h: (0, 0, skip + h))

    outs = pl.pallas_call(
        functools.partial(attention_kernel, layout, depth, pool_size),
        grid=(heads,),
        in_specs=[block_spec(b.shape[0], rows, b.shape[2]) for b in flat]
        + [block_spec(2, extra, coarse.shape[2])],
        out_specs=[block_spec(2, rows, width)] * parts
        + [block_spec(2, own, width), block_spec(2, extra, width)],
        out_shape=[jax.ShapeDtypeStruct((2, rows, width), jnp.bfloat16)] * parts
        + [
            jax.ShapeDtypeStruct((2, own, width), jnp.float32),
            jax.ShapeDtypeStruct((2, extra, width), jnp.float32),
        ],
        compiler_params=pltpu.CompilerParams(vmem_limit_bytes=40 * 1024 * 1024),
        cost_estimate=pl.CostEstimate(
            flops=12 * heads * own * seen * HD,
            bytes_accessed=24 * own * width,
            transcendentals=heads * own * seen,
        ),
        name="attention",
    )(*flat, coarse)
    return outs[:parts], outs[parts], outs[parts + 1]


def on_device(queries, keys_in, values_in, grad_out):
    seq_count = lax.axis_size("seq")
    parts = lax.axis_size("head")
    me = lax.axis_index("head")
    depth = seq_count.bit_length() - 1
    rows, columns = queries.shape
    own = rows * parts
    pool_size = own // CROWS
    per = rows // pool_size
    width = columns // parts
    heads = width // HD
    split = [heads - heads // 2, heads // 2][: min(heads, 2)]
    groups = len(split)
    starts = [sum(split[:g]) for g in range(groups)]
    far = range(2, parts)
    arrays = (keys_in, values_in, queries, grad_out)

    def column(part, head=0):
        return (me ^ part) * width + head * HD

    def slab(part, head, size):
        return jnp.stack(
            [lax.dynamic_slice_in_dim(x, column(part, head), size, axis=1) for x in arrays]
        )

    landed = {}

    def send(block, part, name):
        landed[name] = swapped(block, "head", part)

    def after(block, names):
        for name in names:
            if name in landed:
                block, landed[name] = lax.optimization_barrier((block, landed[name]))
        return block

    def pieces(part, g):
        whole = slab(part, starts[g], split[g] * HD)
        return [whole[:2], whole[2:]] if g == 0 and 2 <= part < 2 + FIRST else [whole]

    slabs = [[pieces(part, g) for part in far] for g in range(groups)]
    slabs[0], keys_now, values_now = lax.optimization_barrier((slabs[0], keys_in, values_in))
    pooled_here = jnp.stack(
        [
            jnp.mean(x.astype(jnp.float32).reshape(per, pool_size, columns), axis=1)
            for x in (keys_now, values_now)
        ]
    )
    pooled_parts = []
    for part in range(parts):
        block = lax.dynamic_slice_in_dim(pooled_here, column(part), width, axis=2)
        pooled_parts.append(swapped(block, "head", part) if part else block)
    for part in far[:FIRST]:
        send(slabs[0][part - 2][0], part, ("in", 0, part, 0))
    mean_now = jnp.concatenate(pooled_parts, axis=1)
    for g in range(groups):
        send(slab(1, starts[g], split[g] * HD), 1, ("near", g))
    siblings = []
    for level in range(depth):
        if level < len(F_PACE):
            mean_now = after(mean_now, F_PACE[level])
        received = swapped(mean_now, "seq", 1 << level)
        siblings.append(received)
        mean_now = 0.5 * (mean_now + received)

    blocks = []
    for g in range(groups):
        if g and IN_GATE:
            at = min(IN_GATE, depth) - 1
            slabs[g], siblings[at] = lax.optimization_barrier((slabs[g], siblings[at]))
        for part in far:
            for at, piece in enumerate(slabs[g][part - 2]):
                if ("in", g, part, at) not in landed:
                    send(piece, part, ("in", g, part, at))
        blocks.append([[slab(0, starts[g], split[g] * HD)], [landed["near", g]]])
    coarse = jnp.concatenate(siblings, axis=1).astype(jnp.bfloat16)

    kept, grads, sums = [], [], []
    for g in range(groups):
        blocks[g][1] = [landed["near", g]]
        here = blocks[g] + [
            [landed["in", g, part, at] for at in range(len(slabs[g][part - 2]))] for part in far
        ]
        sent, local, coarse_grad = attention(here, coarse, starts[g], split[g], depth, pool_size)
        kept.append(sent)
        grads.append(local)
        sums.append(coarse_grad.reshape(2, depth, CROWS, split[g] * HD))
        for part in far:
            send(sent[part], part, ("mid", g, part))

    def chain(coarse_grad, pace):
        pace = list(pace) + [()] * depth
        coarse_grad = after(coarse_grad, pace[0])
        above = jnp.zeros(coarse_grad[:, 0].shape, jnp.float32)
        for level in reversed(range(depth)):
            outgoing = coarse_grad[:, level] + 0.5 * above
            received = swapped(outgoing.astype(jnp.bfloat16), "seq", 1 << level)
            received = after(received, pace[depth - level])
            above = 0.5 * above + received.astype(jnp.float32)
        return above / float(pool_size)

    def total(part, local, above):
        spread = jnp.repeat(above[:, part * per : (part + 1) * per], pool_size, axis=1)
        return (local[:, part * rows : (part + 1) * rows] + spread).astype(jnp.bfloat16)

    own_last, near_last = [], []
    for g in range(groups):
        above = chain(sums[g], (PACE0, PACE1)[g])
        for part in far:
            send(total(part, grads[g], above), part, ("last", g, part))
        own_last.append(total(0, grads[g], above))
        near_last.append(total(1, grads[g], above))
    near = [swapped(kept[g][1], "head", 1) for g in range(groups)]
    near_last = [swapped(block, "head", 1) for block in near_last]

    outs = [jnp.zeros((rows, columns), jnp.bfloat16) for _ in range(4)]

    def place(first, back, part, head=0):
        for which in range(back.shape[0]):
            outs[first + which] = lax.dynamic_update_slice(
                outs[first + which], back[which], (0, column(part, head))
            )

    for g in range(groups):
        place(0, kept[g][0], 0, starts[g])
        place(0, near[g], 1, starts[g])
        place(2, own_last[g], 0, starts[g])
        place(2, near_last[g], 1, starts[g])
        for part in far:
            place(0, landed["mid", g, part], part, starts[g])
            place(2, landed["last", g, part], part, starts[g])
    return tuple(outs)


def solution(mesh):
    placed = (P(("seq", "head"), None),) * 4
    return jax.shard_map(
        on_device, mesh=mesh, in_specs=placed, out_specs=placed, check_vma=False
    )
```

```python
import functools
import math

import jax
import jax.numpy as jnp
from jax import lax
from jax.experimental import pallas as pl
from jax.experimental.pallas import tpu as pltpu
from jax.sharding import PartitionSpec as P

HD = 128
CROWS = 16
SCALE = HD**-0.5
PACE = (
    (),
    ((("mid", 0, 2),), (("mid", 0, 3),), (("last", 0, 2),), (("last", 0, 3),)),
)
PACE_IN = ((("in", 0, 2, 0),), (), (("near", 1),))


def swapped(block, axis, mask):
    count = lax.axis_size(axis)
    return lax.ppermute(block, axis, [(i, i ^ mask) for i in range(count)])


def attention_kernel(layout, depth, pool_size, *refs):
    parts, count = len(layout), sum(len(sizes) for sizes in layout)
    blocks, at = [], 0
    for sizes in layout:
        blocks.append([(ref, i) for ref, size in zip(refs[at:], sizes) for i in range(size)])
        at += len(sizes)
    coarse_ref = refs[count]
    out_refs = refs[count + 1 : count + 1 + parts]
    local_ref, coarse_grad_ref = refs[count + 1 + parts :]
    rows = refs[0].shape[1]
    own = parts * rows

    def whole(which):
        return jnp.concatenate([block[which][0][block[which][1]] for block in blocks], axis=0)

    keys = jnp.concatenate([whole(0), coarse_ref[0]], axis=0)
    values = jnp.concatenate([whole(1), coarse_ref[1]], axis=0)
    queries, grads = whole(2), whole(3)
    seen = keys.shape[0]

    def dot(a, b, over):
        return lax.dot_general(
            a, b, (((over[0],), (over[1],)), ((), ())), preferred_element_type=jnp.float32
        )

    scores = dot(keys, queries, (1, 1)) * (SCALE * math.log2(math.e))
    row = lax.broadcasted_iota(jnp.int32, (seen - own, 1), 0)
    offset = (row // CROWS).astype(jnp.float32) + math.log2(pool_size)
    scores = jnp.concatenate([scores[:own], scores[own:] + offset], axis=0)
    powers = jnp.exp2(scores - jnp.max(scores, axis=0, keepdims=True))
    probs = powers * (1.0 / jnp.sum(powers, axis=0, keepdims=True))
    probs_low = probs.astype(jnp.bfloat16)
    dprob = dot(values, grads, (1, 1))
    mean = jnp.sum(probs * dprob, axis=0, keepdims=True)
    dscore = (probs * SCALE * (dprob - mean)).astype(jnp.bfloat16)
    attended = dot(values, probs_low, (0, 0)).T.astype(jnp.bfloat16)
    grad_query = dot(keys, dscore, (0, 0)).T.astype(jnp.bfloat16)
    dkeys = dot(dscore, queries, (1, 0))
    dvalues = dot(probs_low, grads, (1, 0))
    for part in range(parts):
        here = slice(part * rows, (part + 1) * rows)
        out_refs[part][0] = attended[here]
        out_refs[part][1] = grad_query[here]
    local_ref[0] = dkeys[:own]
    local_ref[1] = dvalues[:own]
    coarse_grad_ref[0] = dkeys[own:]
    coarse_grad_ref[1] = dvalues[own:]


def attention(blocks, coarse, first, heads, depth, pool_size):
    parts = len(blocks)
    layout = tuple(tuple(piece.shape[0] for piece in pieces) for pieces in blocks)
    flat = [piece for pieces in blocks for piece in pieces]
    rows = flat[0].shape[1]
    width = heads * HD
    own = parts * rows
    extra = coarse.shape[1]
    seen = own + extra

    def block_spec(lead, height, total):
        skip = first if total > width else 0
        return pl.BlockSpec((lead, height, HD), lambda h: (0, 0, skip + h))

    outs = pl.pallas_call(
        functools.partial(attention_kernel, layout, depth, pool_size),
        grid=(heads,),
        in_specs=[block_spec(b.shape[0], rows, b.shape[2]) for b in flat]
        + [block_spec(2, extra, coarse.shape[2])],
        out_specs=[block_spec(2, rows, width)] * parts
        + [block_spec(2, own, width), block_spec(2, extra, width)],
        out_shape=[jax.ShapeDtypeStruct((2, rows, width), jnp.bfloat16)] * parts
        + [
            jax.ShapeDtypeStruct((2, own, width), jnp.float32),
            jax.ShapeDtypeStruct((2, extra, width), jnp.float32),
        ],
        compiler_params=pltpu.CompilerParams(vmem_limit_bytes=40 * 1024 * 1024),
        cost_estimate=pl.CostEstimate(
            flops=12 * heads * own * seen * HD,
            bytes_accessed=24 * own * width,
            transcendentals=heads * own * seen,
        ),
        name="attention",
    )(*flat, coarse)
    return outs[:parts], outs[parts], outs[parts + 1]


def on_device(queries, keys_in, values_in, grad_out):
    seq_count = lax.axis_size("seq")
    parts = lax.axis_size("head")
    me = lax.axis_index("head")
    depth = seq_count.bit_length() - 1
    rows, columns = queries.shape
    own = rows * parts
    pool_size = own // CROWS
    per = rows // pool_size
    width = columns // parts
    heads = width // HD
    split = [heads - heads // 2, heads // 2][: min(heads, 2)]
    groups = len(split)
    starts = [sum(split[:g]) for g in range(groups)]
    far = range(2, parts)
    arrays = (keys_in, values_in, queries, grad_out)

    def column(part, head=0):
        return (me ^ part) * width + head * HD

    def slab(part, head, size):
        return jnp.stack(
            [lax.dynamic_slice_in_dim(x, column(part, head), size, axis=1) for x in arrays]
        )

    landed = {}

    def send(block, part, name):
        landed[name] = swapped(block, "head", part)

    def after(block, names):
        for name in names:
            if name in landed:
                block, landed[name] = lax.optimization_barrier((block, landed[name]))
        return block

    def pieces(part, g):
        whole = slab(part, starts[g], split[g] * HD)
        return [whole[:2], whole[2:]] if g == 0 and part == 2 else [whole]

    both = jnp.concatenate([keys_in, values_in])
    opening = lax.dynamic_slice_in_dim(both, column(2), split[0] * HD, axis=1)
    opening = opening.reshape(2, rows, split[0] * HD)
    keys_in, values_in = lax.optimization_barrier((keys_in, values_in))
    arrays = (keys_in, values_in, queries, grad_out)
    slabs = [[pieces(part, g) for part in far] for g in range(groups)]
    others = (slabs[0][0][1:], slabs[0][1:])
    others, keys_now, values_now = lax.optimization_barrier((others, keys_in, values_in))
    slabs[0] = [[opening, *others[0]], *others[1]]
    pooled_here = jnp.stack(
        [
            jnp.mean(x.astype(jnp.float32).reshape(per, pool_size, columns), axis=1)
            for x in (keys_now, values_now)
        ]
    )
    pooled_parts = []
    for part in range(parts):
        block = lax.dynamic_slice_in_dim(pooled_here, column(part), width, axis=2)
        pooled_parts.append(swapped(block, "head", part) if part else block)
    send(slabs[0][0][0], 2, ("in", 0, 2, 0))
    mean_now = jnp.concatenate(pooled_parts, axis=1)
    for g in range(groups):
        send(slab(1, starts[g], split[g] * HD), 1, ("near", g))
    siblings = []
    for level in range(depth):
        if level < len(PACE_IN):
            mean_now = after(mean_now, PACE_IN[level])
        received = swapped(mean_now, "seq", 1 << level)
        siblings.append(received)
        mean_now = 0.5 * (mean_now + received)

    blocks = []
    for g in range(groups):
        if g:
            at = min(2, depth) - 1
            slabs[g], siblings[at] = lax.optimization_barrier((slabs[g], siblings[at]))
        for part in far:
            for at, piece in enumerate(slabs[g][part - 2]):
                if ("in", g, part, at) not in landed:
                    send(piece, part, ("in", g, part, at))
        blocks.append([[slab(0, starts[g], split[g] * HD)], [landed["near", g]]])
    coarse = jnp.concatenate(siblings, axis=1).astype(jnp.bfloat16)

    kept, grads, sums = [], [], []
    for g in range(groups):
        blocks[g][1] = [landed["near", g]]
        here = blocks[g] + [
            [landed["in", g, part, at] for at in range(len(slabs[g][part - 2]))] for part in far
        ]
        sent, local, coarse_grad = attention(here, coarse, starts[g], split[g], depth, pool_size)
        kept.append(sent)
        grads.append(local)
        sums.append(coarse_grad.reshape(2, depth, CROWS, split[g] * HD))
        for part in far:
            send(sent[part], part, ("mid", g, part))

    def chain(coarse_grad, pace):
        pace = list(pace) + [()] * (depth + 1)
        coarse_grad = after(coarse_grad, pace[0])
        above = jnp.zeros(coarse_grad[:, 0].shape, jnp.float32)
        for level in reversed(range(depth)):
            outgoing = coarse_grad[:, level] + 0.5 * above
            received = swapped(outgoing.astype(jnp.bfloat16), "seq", 1 << level)
            received = after(received, pace[depth - level])
            above = 0.5 * above + received.astype(jnp.float32)
        return above / float(pool_size)

    def total(part, local, above):
        spread = jnp.repeat(above[:, part * per : (part + 1) * per], pool_size, axis=1)
        return (local[:, part * rows : (part + 1) * rows] + spread).astype(jnp.bfloat16)

    own_last, near_last = [], []
    for g in range(groups):
        above = chain(sums[g], PACE[g])
        for part in far:
            send(total(part, grads[g], above), part, ("last", g, part))
        own_last.append(total(0, grads[g], above))
        near_last.append(total(1, grads[g], above))
    near = [swapped(kept[g][1], "head", 1) for g in range(groups)]
    near_last = [swapped(block, "head", 1) for block in near_last]

    outs = [jnp.zeros((rows, columns), jnp.bfloat16) for _ in range(4)]

    def place(first, back, part, head=0):
        for which in range(back.shape[0]):
            outs[first + which] = lax.dynamic_update_slice(
                outs[first + which], back[which], (0, column(part, head))
            )

    for g in range(groups):
        place(0, kept[g][0], 0, starts[g])
        place(0, near[g], 1, starts[g])
        place(2, own_last[g], 0, starts[g])
        place(2, near_last[g], 1, starts[g])
        for part in far:
            place(0, landed["mid", g, part], part, starts[g])
            place(2, landed["last", g, part], part, starts[g])
    return tuple(outs)


def solution(mesh):
    placed = (P(("seq", "head"), None),) * 4
    return jax.shard_map(
        on_device, mesh=mesh, in_specs=placed, out_specs=placed, check_vma=False
    )
```

```python
import functools
import math

import jax
import jax.numpy as jnp
from jax import lax
from jax.experimental import pallas as pl
from jax.experimental.pallas import tpu as pltpu
from jax.sharding import PartitionSpec as P

HD = 128
CROWS = 16
SCALE = HD**-0.5
LOW = ((2,), ())
PACE = (
    (),
    ((("mid", 0, 2),), (("mid", 0, 3),), (("last", 0, 2),), (("last", 0, 3),)),
)
PACE_IN = ((("in", 0, 2, 0),), (), (("near", 1),))


def swapped(block, axis, mask):
    count = lax.axis_size(axis)
    return lax.ppermute(block, axis, [(i, i ^ mask) for i in range(count)])


def attention_kernel(layout, depth, pool_size, *refs):
    parts, count = len(layout), sum(len(sizes) for sizes in layout)
    blocks, at = [], 0
    for sizes in layout:
        blocks.append([(ref, i) for ref, size in zip(refs[at:], sizes) for i in range(size)])
        at += len(sizes)
    coarse_ref = refs[count]
    out_refs = refs[count + 1 : count + 1 + parts]
    local_ref, coarse_grad_ref = refs[count + 1 + parts :]
    rows = refs[0].shape[1]
    own = parts * rows

    def whole(which):
        return jnp.concatenate([block[which][0][block[which][1]] for block in blocks], axis=0)

    keys = jnp.concatenate([whole(0), coarse_ref[0]], axis=0)
    values = jnp.concatenate([whole(1), coarse_ref[1]], axis=0)
    queries, grads = whole(2), whole(3)
    seen = keys.shape[0]

    def dot(a, b, over):
        return lax.dot_general(
            a, b, (((over[0],), (over[1],)), ((), ())), preferred_element_type=jnp.float32
        )

    scores = dot(keys, queries, (1, 1)) * (SCALE * math.log2(math.e))
    row = lax.broadcasted_iota(jnp.int32, (seen - own, 1), 0)
    offset = (row // CROWS).astype(jnp.float32) + math.log2(pool_size)
    scores = jnp.concatenate([scores[:own], scores[own:] + offset], axis=0)
    powers = jnp.exp2(scores - jnp.max(scores, axis=0, keepdims=True))
    probs = powers * (1.0 / jnp.sum(powers, axis=0, keepdims=True))
    probs_low = probs.astype(jnp.bfloat16)
    dprob = dot(values, grads, (1, 1))
    mean = jnp.sum(probs * dprob, axis=0, keepdims=True)
    dscore = (probs * SCALE * (dprob - mean)).astype(jnp.bfloat16)
    attended = dot(values, probs_low, (0, 0)).T.astype(jnp.bfloat16)
    grad_query = dot(keys, dscore, (0, 0)).T.astype(jnp.bfloat16)
    dkeys = dot(dscore, queries, (1, 0))
    dvalues = dot(probs_low, grads, (1, 0))
    for part in range(parts):
        here = slice(part * rows, (part + 1) * rows)
        out_refs[part][0] = attended[here]
        out_refs[part][1] = grad_query[here]
    local_ref[0] = dkeys[:own]
    local_ref[1] = dvalues[:own]
    coarse_grad_ref[0] = dkeys[own:]
    coarse_grad_ref[1] = dvalues[own:]


def attention(blocks, coarse, first, heads, depth, pool_size):
    parts = len(blocks)
    layout = tuple(tuple(piece.shape[0] for piece in pieces) for pieces in blocks)
    flat = [piece for pieces in blocks for piece in pieces]
    rows = flat[0].shape[1]
    width = heads * HD
    own = parts * rows
    extra = coarse.shape[1]
    seen = own + extra

    def block_spec(lead, height, total):
        skip = first if total > width else 0
        return pl.BlockSpec((lead, height, HD), lambda h: (0, 0, skip + h))

    outs = pl.pallas_call(
        functools.partial(attention_kernel, layout, depth, pool_size),
        grid=(heads,),
        in_specs=[block_spec(b.shape[0], rows, b.shape[2]) for b in flat]
        + [block_spec(2, extra, coarse.shape[2])],
        out_specs=[block_spec(2, rows, width)] * parts
        + [block_spec(2, own, width), block_spec(2, extra, width)],
        out_shape=[jax.ShapeDtypeStruct((2, rows, width), jnp.bfloat16)] * parts
        + [
            jax.ShapeDtypeStruct((2, own, width), jnp.float32),
            jax.ShapeDtypeStruct((2, extra, width), jnp.float32),
        ],
        compiler_params=pltpu.CompilerParams(vmem_limit_bytes=40 * 1024 * 1024),
        cost_estimate=pl.CostEstimate(
            flops=12 * heads * own * seen * HD,
            bytes_accessed=24 * own * width,
            transcendentals=heads * own * seen,
        ),
        name="attention",
    )(*flat, coarse)
    return outs[:parts], outs[parts], outs[parts + 1]


def on_device(queries, keys_in, values_in, grad_out):
    seq_count = lax.axis_size("seq")
    parts = lax.axis_size("head")
    me = lax.axis_index("head")
    depth = seq_count.bit_length() - 1
    rows, columns = queries.shape
    own = rows * parts
    pool_size = own // CROWS
    per = rows // pool_size
    width = columns // parts
    heads = width // HD
    split = [heads - heads // 2, heads // 2][: min(heads, 2)]
    groups = len(split)
    starts = [sum(split[:g]) for g in range(groups)]
    far = range(2, parts)
    arrays = (keys_in, values_in, queries, grad_out)

    def column(part, head=0):
        return (me ^ part) * width + head * HD

    def slab(part, head, size):
        return jnp.stack(
            [lax.dynamic_slice_in_dim(x, column(part, head), size, axis=1) for x in arrays]
        )

    landed = {}

    def send(block, part, name):
        landed[name] = swapped(block, "head", part)

    def after(block, names):
        for name in names:
            if name in landed:
                block, landed[name] = lax.optimization_barrier((block, landed[name]))
        return block

    def pieces(part, g):
        whole = slab(part, starts[g], split[g] * HD)
        return [whole[:2], whole[2:]] if g == 0 and part == 2 else [whole]

    both = jnp.concatenate([keys_in, values_in])
    opening = lax.dynamic_slice_in_dim(both, column(2), split[0] * HD, axis=1)
    opening = opening.reshape(2, rows, split[0] * HD)
    keys_in, values_in = lax.optimization_barrier((keys_in, values_in))
    arrays = (keys_in, values_in, queries, grad_out)
    slabs = [[pieces(part, g) for part in far] for g in range(groups)]
    others = (slabs[0][0][1:], slabs[0][1:])
    others, keys_now, values_now = lax.optimization_barrier((others, keys_in, values_in))
    slabs[0] = [[opening, *others[0]], *others[1]]
    pooled_here = jnp.stack(
        [
            jnp.mean(x.astype(jnp.float32).reshape(per, pool_size, columns), axis=1)
            for x in (keys_now, values_now)
        ]
    )
    pooled_parts = []
    for part in range(parts):
        block = lax.dynamic_slice_in_dim(pooled_here, column(part), width, axis=2)
        pooled_parts.append(swapped(block, "head", part) if part else block)
    send(slabs[0][0][0], 2, ("in", 0, 2, 0))
    mean_now = jnp.concatenate(pooled_parts, axis=1)
    for g in range(groups):
        send(slab(1, starts[g], split[g] * HD), 1, ("near", g))
    siblings = []
    for level in range(depth):
        if level < len(PACE_IN):
            mean_now = after(mean_now, PACE_IN[level])
        received = swapped(mean_now, "seq", 1 << level)
        siblings.append(received)
        mean_now = 0.5 * (mean_now + received)

    blocks = []
    for g in range(groups):
        if g:
            at = min(2, depth) - 1
            slabs[g], siblings[at] = lax.optimization_barrier((slabs[g], siblings[at]))
        for part in far:
            for at, piece in enumerate(slabs[g][part - 2]):
                if ("in", g, part, at) not in landed:
                    send(piece, part, ("in", g, part, at))
        blocks.append([[slab(0, starts[g], split[g] * HD)], [landed["near", g]]])
    coarse = jnp.concatenate(siblings, axis=1).astype(jnp.bfloat16)

    kept, grads, sums = [], [], []
    for g in range(groups):
        blocks[g][1] = [landed["near", g]]
        here = blocks[g] + [
            [landed["in", g, part, at] for at in range(len(slabs[g][part - 2]))] for part in far
        ]
        sent, local, coarse_grad = attention(here, coarse, starts[g], split[g], depth, pool_size)
        kept.append(sent)
        grads.append(local)
        sums.append(coarse_grad.reshape(2, depth, CROWS, split[g] * HD))
        for part in far:
            send(sent[part], part, ("mid", g, part))

    def chain(coarse_grad, pace, low):
        pace = list(pace) + [()] * (depth + 1)
        coarse_grad = after(coarse_grad, pace[0])
        above = jnp.zeros(coarse_grad[:, 0].shape, jnp.float32)
        for level in reversed(range(depth)):
            outgoing = coarse_grad[:, level] + 0.5 * above
            if level in low:
                outgoing = outgoing.astype(jnp.bfloat16)
            received = swapped(outgoing, "seq", 1 << level)
            received = after(received, pace[depth - level])
            above = 0.5 * above + received.astype(jnp.float32)
        return above / float(pool_size)

    def total(part, local, above):
        spread = jnp.repeat(above[:, part * per : (part + 1) * per], pool_size, axis=1)
        return (local[:, part * rows : (part + 1) * rows] + spread).astype(jnp.bfloat16)

    own_last, near_last = [], []
    for g in range(groups):
        above = chain(sums[g], PACE[g], LOW[g])
        for part in far:
            block = total(part, grads[g], above)
            if g == groups - 1:
                send(block[:1], part, ("last", g, part, 0))
                send(block[1:], part, ("last", g, part, 1))
            else:
                send(block, part, ("last", g, part))
        own_last.append(total(0, grads[g], above))
        near_last.append(total(1, grads[g], above))
    near = [swapped(kept[g][1], "head", 1) for g in range(groups)]
    near_last = [swapped(block, "head", 1) for block in near_last]

    outs = [jnp.zeros((rows, columns), jnp.bfloat16) for _ in range(4)]

    def place(first, back, part, head=0):
        for which in range(back.shape[0]):
            outs[first + which] = lax.dynamic_update_slice(
                outs[first + which], back[which], (0, column(part, head))
            )

    for g in range(groups):
        place(0, kept[g][0], 0, starts[g])
        place(0, near[g], 1, starts[g])
        place(2, own_last[g], 0, starts[g])
        place(2, near_last[g], 1, starts[g])
        for part in far:
            place(0, landed["mid", g, part], part, starts[g])
            if g == groups - 1:
                place(2, landed["last", g, part, 0], part, starts[g])
                place(3, landed["last", g, part, 1], part, starts[g])
            else:
                place(2, landed["last", g, part], part, starts[g])
    return tuple(outs)


def solution(mesh):
    placed = (P(("seq", "head"), None),) * 4
    return jax.shard_map(
        on_device, mesh=mesh, in_specs=placed, out_specs=placed, check_vma=False
    )
```

```python
import functools
import math

import jax
import jax.numpy as jnp
from jax import lax
from jax.experimental import pallas as pl
from jax.experimental.pallas import tpu as pltpu
from jax.sharding import PartitionSpec as P

HD = 128
CROWS = 16
SCALE = HD**-0.5
LOW = ((2,), ())
PACE = (
    (),
    ((("mid", 0, 2),), (("mid", 0, 3),), (("last", 0, 2),), (("last", 0, 3),)),
)
PACE_IN = ((("in", 0, 2, 0),), (), (("near", 1),))


def swapped(block, axis, mask):
    count = lax.axis_size(axis)
    return lax.ppermute(block, axis, [(i, i ^ mask) for i in range(count)])


def attention_kernel(layout, depth, pool_size, *refs):
    parts, count = len(layout), sum(len(sizes) for sizes in layout)
    blocks, at = [], 0
    for sizes in layout:
        blocks.append([(ref, i) for ref, size in zip(refs[at:], sizes) for i in range(size)])
        at += len(sizes)
    coarse_ref = refs[count]
    out_refs = refs[count + 1 : count + 1 + parts]
    local_ref, coarse_grad_ref = refs[count + 1 + parts :]
    rows = refs[0].shape[1]
    own = parts * rows

    def whole(which):
        return jnp.concatenate([block[which][0][block[which][1]] for block in blocks], axis=0)

    keys = jnp.concatenate([whole(0), coarse_ref[0]], axis=0)
    values = jnp.concatenate([whole(1), coarse_ref[1]], axis=0)
    queries, grads = whole(2), whole(3)
    seen = keys.shape[0]

    def dot(a, b, over):
        return lax.dot_general(
            a, b, (((over[0],), (over[1],)), ((), ())), preferred_element_type=jnp.float32
        )

    scores = dot(keys, queries, (1, 1)) * (SCALE * math.log2(math.e))
    row = lax.broadcasted_iota(jnp.int32, (seen - own, 1), 0)
    offset = (row // CROWS).astype(jnp.float32) + math.log2(pool_size)
    scores = jnp.concatenate([scores[:own], scores[own:] + offset], axis=0)
    powers = jnp.exp2(scores - jnp.max(scores, axis=0, keepdims=True))
    probs = powers * (1.0 / jnp.sum(powers, axis=0, keepdims=True))
    probs_low = probs.astype(jnp.bfloat16)
    dprob = dot(values, grads, (1, 1))
    mean = jnp.sum(probs * dprob, axis=0, keepdims=True)
    dscore = (probs * SCALE * (dprob - mean)).astype(jnp.bfloat16)
    attended = dot(values, probs_low, (0, 0)).T.astype(jnp.bfloat16)
    grad_query = dot(keys, dscore, (0, 0)).T.astype(jnp.bfloat16)
    dkeys = dot(dscore, queries, (1, 0))
    dvalues = dot(probs_low, grads, (1, 0))
    for part in range(parts):
        here = slice(part * rows, (part + 1) * rows)
        out_refs[part][0] = attended[here]
        out_refs[part][1] = grad_query[here]
    local_ref[0] = dkeys[:own]
    local_ref[1] = dvalues[:own]
    coarse_grad_ref[0] = dkeys[own:]
    coarse_grad_ref[1] = dvalues[own:]


def attention(blocks, coarse, first, heads, depth, pool_size):
    parts = len(blocks)
    layout = tuple(tuple(piece.shape[0] for piece in pieces) for pieces in blocks)
    flat = [piece for pieces in blocks for piece in pieces]
    rows = flat[0].shape[1]
    width = heads * HD
    own = parts * rows
    extra = coarse.shape[1]
    seen = own + extra

    def block_spec(lead, height, total):
        skip = first if total > width else 0
        return pl.BlockSpec((lead, height, HD), lambda h: (0, 0, skip + h))

    outs = pl.pallas_call(
        functools.partial(attention_kernel, layout, depth, pool_size),
        grid=(heads,),
        in_specs=[block_spec(b.shape[0], rows, b.shape[2]) for b in flat]
        + [block_spec(2, extra, coarse.shape[2])],
        out_specs=[block_spec(2, rows, width)] * parts
        + [block_spec(2, own, width), block_spec(2, extra, width)],
        out_shape=[jax.ShapeDtypeStruct((2, rows, width), jnp.bfloat16)] * parts
        + [
            jax.ShapeDtypeStruct((2, own, width), jnp.float32),
            jax.ShapeDtypeStruct((2, extra, width), jnp.float32),
        ],
        compiler_params=pltpu.CompilerParams(vmem_limit_bytes=40 * 1024 * 1024),
        cost_estimate=pl.CostEstimate(
            flops=12 * heads * own * seen * HD,
            bytes_accessed=24 * own * width,
            transcendentals=heads * own * seen,
        ),
        name="attention",
    )(*flat, coarse)
    return outs[:parts], outs[parts], outs[parts + 1]


def held(array):
    hbm = pl.BlockSpec(memory_space=pltpu.HBM)
    return pl.pallas_call(
        lambda *refs: None,
        in_specs=[hbm],
        out_specs=hbm,
        out_shape=jax.ShapeDtypeStruct(array.shape, array.dtype),
        input_output_aliases={0: 0},
        name="held",
    )(array)


def on_device(queries, keys_in, values_in, grad_out):
    seq_count = lax.axis_size("seq")
    parts = lax.axis_size("head")
    me = lax.axis_index("head")
    depth = seq_count.bit_length() - 1
    rows, columns = queries.shape
    own = rows * parts
    pool_size = own // CROWS
    per = rows // pool_size
    width = columns // parts
    heads = width // HD
    split = [heads - heads // 2, heads // 2][: min(heads, 2)]
    groups = len(split)
    starts = [sum(split[:g]) for g in range(groups)]
    far = range(2, parts)
    arrays = (keys_in, values_in, queries, grad_out)

    def column(part, head=0):
        return (me ^ part) * width + head * HD

    def slab(part, head, size):
        return jnp.stack(
            [lax.dynamic_slice_in_dim(x, column(part, head), size, axis=1) for x in arrays]
        )

    landed = {}

    def send(block, part, name):
        landed[name] = swapped(block, "head", part)

    def after(block, names):
        for name in names:
            if name in landed:
                block, landed[name] = lax.optimization_barrier((block, landed[name]))
        return block

    def pieces(part, g):
        whole = slab(part, starts[g], split[g] * HD)
        return [whole[:2], whole[2:]] if g == 0 and part == 2 else [whole]

    both = jnp.concatenate([keys_in, values_in])
    opening = lax.dynamic_slice_in_dim(both, column(2), split[0] * HD, axis=1)
    opening = opening.reshape(2, rows, split[0] * HD)
    keys_in, values_in = lax.optimization_barrier((keys_in, values_in))
    arrays = (keys_in, values_in, queries, grad_out)
    slabs = [[pieces(part, g) for part in far] for g in range(groups)]
    others = (slabs[0][0][1:], slabs[0][1:])
    others, keys_now, values_now = lax.optimization_barrier((others, keys_in, values_in))
    slabs[0] = [[opening, *others[0]], *others[1]]
    pooled_here = jnp.stack(
        [
            jnp.mean(x.astype(jnp.float32).reshape(per, pool_size, columns), axis=1)
            for x in (keys_now, values_now)
        ]
    )
    pooled_parts = []
    for part in range(parts):
        block = lax.dynamic_slice_in_dim(pooled_here, column(part), width, axis=2)
        pooled_parts.append(swapped(block, "head", part) if part else block)
    send(slabs[0][0][0], 2, ("in", 0, 2, 0))
    mean_now = jnp.concatenate(pooled_parts, axis=1)
    for g in range(groups):
        send(slab(1, starts[g], split[g] * HD), 1, ("near", g))
    siblings = []
    for level in range(depth):
        if level < len(PACE_IN):
            mean_now = after(mean_now, PACE_IN[level])
        received = swapped(mean_now, "seq", 1 << level)
        siblings.append(received)
        mean_now = 0.5 * (mean_now + received)

    blocks = []
    for g in range(groups):
        if g:
            at = min(2, depth) - 1
            slabs[g], siblings[at] = lax.optimization_barrier((slabs[g], siblings[at]))
        for part in far:
            for at, piece in enumerate(slabs[g][part - 2]):
                if ("in", g, part, at) not in landed:
                    send(piece, part, ("in", g, part, at))
        blocks.append([[slab(0, starts[g], split[g] * HD)], [landed["near", g]]])
    coarse = jnp.concatenate(siblings, axis=1).astype(jnp.bfloat16)

    kept, grads, sums = [], [], []
    for g in range(groups):
        blocks[g][1] = [landed["near", g]]
        here = blocks[g] + [
            [landed["in", g, part, at] for at in range(len(slabs[g][part - 2]))] for part in far
        ]
        sent, local, coarse_grad = attention(here, coarse, starts[g], split[g], depth, pool_size)
        kept.append(sent)
        grads.append(local)
        sums.append(coarse_grad.reshape(2, depth, CROWS, split[g] * HD))
        for part in far:
            send(sent[part], part, ("mid", g, part))

    def chain(coarse_grad, pace, low):
        pace = list(pace) + [()] * (depth + 1)
        coarse_grad = after(coarse_grad, pace[0])
        above = jnp.zeros(coarse_grad[:, 0].shape, jnp.float32)
        for level in reversed(range(depth)):
            outgoing = coarse_grad[:, level] + 0.5 * above
            if level in low:
                outgoing = outgoing.astype(jnp.bfloat16)
            received = swapped(outgoing, "seq", 1 << level)
            received = after(received, pace[depth - level])
            above = 0.5 * above + received.astype(jnp.float32)
        return above / float(pool_size)

    def total(part, local, above):
        spread = jnp.repeat(above[:, part * per : (part + 1) * per], pool_size, axis=1)
        return (local[:, part * rows : (part + 1) * rows] + spread).astype(jnp.bfloat16)

    own_last, near_last = [], []
    for g in range(groups):
        above = chain(sums[g], PACE[g], LOW[g])
        for part in far:
            block = total(part, grads[g], above)
            if g == groups - 1:
                send(block[:1], part, ("last", g, part, 0))
                send(block[1:], part, ("last", g, part, 1))
            else:
                send(block, part, ("last", g, part))
        own_last.append(total(0, grads[g], above))
        near_last.append(total(1, grads[g], above))
    near = [swapped(kept[g][1], "head", 1) for g in range(groups)]
    near_last = [swapped(block, "head", 1) for block in near_last]

    outs = [jnp.zeros((rows, columns), jnp.bfloat16) for _ in range(4)]

    def place(first, back, part, head=0):
        for which in range(back.shape[0]):
            outs[first + which] = lax.dynamic_update_slice(
                outs[first + which], back[which], (0, column(part, head))
            )

    for g in range(groups):
        place(0, kept[g][0], 0, starts[g])
        place(0, near[g], 1, starts[g])
        place(2, own_last[g], 0, starts[g])
        place(2, near_last[g], 1, starts[g])
        for part in far:
            place(0, landed["mid", g, part], part, starts[g])
            if g < groups - 1:
                place(2, landed["last", g, part], part, starts[g])
            else:
                place(2, landed["last", g, part, 0], part, starts[g])
    for at, part in enumerate(far):
        if at == 1:
            outs[3] = held(outs[3])
        place(3, landed["last", groups - 1, part, 1], part, starts[-1])
    return tuple(outs)


def solution(mesh):
    placed = (P(("seq", "head"), None),) * 4
    return jax.shard_map(
        on_device, mesh=mesh, in_specs=placed, out_specs=placed, check_vma=False
    )
```

```python
import functools
import math

import jax
import jax.numpy as jnp
from jax import lax
from jax.experimental import pallas as pl
from jax.experimental.pallas import tpu as pltpu
from jax.sharding import PartitionSpec as P

HD = 128
CROWS = 16
SCALE = HD**-0.5
LOW = ((2,), ())
PACE = (
    (),
    ((("mid", 0, 2),), (("mid", 0, 3),), (("last", 0, 2),), (("last", 0, 3),)),
)
PACE_IN = ((("in", 0, 2, 0),), (), (("near", 1),))


def swapped(block, axis, mask):
    count = lax.axis_size(axis)
    return lax.ppermute(block, axis, [(i, i ^ mask) for i in range(count)])


def attention_kernel(layout, depth, pool_size, *refs):
    parts, count = len(layout), sum(len(sizes) for sizes in layout)
    blocks, at = [], 0
    for sizes in layout:
        blocks.append([(ref, i) for ref, size in zip(refs[at:], sizes) for i in range(size)])
        at += len(sizes)
    coarse_ref = refs[count]
    out_refs = refs[count + 1 : count + 1 + parts]
    local_ref, coarse_grad_ref = refs[count + 1 + parts :]
    rows = refs[0].shape[1]
    own = parts * rows

    def whole(which):
        return jnp.concatenate([block[which][0][block[which][1]] for block in blocks], axis=0)

    keys = jnp.concatenate([whole(0), coarse_ref[0]], axis=0)
    values = jnp.concatenate([whole(1), coarse_ref[1]], axis=0)
    queries, grads = whole(2), whole(3)
    seen = keys.shape[0]

    def dot(a, b, over):
        return lax.dot_general(
            a, b, (((over[0],), (over[1],)), ((), ())), preferred_element_type=jnp.float32
        )

    scores = dot(keys, queries, (1, 1)) * (SCALE * math.log2(math.e))
    row = lax.broadcasted_iota(jnp.int32, (seen - own, 1), 0)
    offset = (row // CROWS).astype(jnp.float32) + math.log2(pool_size)
    scores = jnp.concatenate([scores[:own], scores[own:] + offset], axis=0)
    powers = jnp.exp2(scores - jnp.max(scores, axis=0, keepdims=True))
    probs = powers * (1.0 / jnp.sum(powers, axis=0, keepdims=True))
    probs_low = probs.astype(jnp.bfloat16)
    dprob = dot(values, grads, (1, 1))
    mean = jnp.sum(probs * dprob, axis=0, keepdims=True)
    dscore = (probs * SCALE * (dprob - mean)).astype(jnp.bfloat16)
    attended = dot(values, probs_low, (0, 0)).T.astype(jnp.bfloat16)
    grad_query = dot(keys, dscore, (0, 0)).T.astype(jnp.bfloat16)
    dkeys = dot(dscore, queries, (1, 0))
    dvalues = dot(probs_low, grads, (1, 0))
    for part in range(parts):
        here = slice(part * rows, (part + 1) * rows)
        out_refs[part][0] = attended[here]
        out_refs[part][1] = grad_query[here]
    local_ref[0] = dkeys[:own]
    local_ref[1] = dvalues[:own]
    coarse_grad_ref[0] = dkeys[own:]
    coarse_grad_ref[1] = dvalues[own:]


def attention(blocks, coarse, first, heads, depth, pool_size):
    parts = len(blocks)
    layout = tuple(tuple(piece.shape[0] for piece in pieces) for pieces in blocks)
    flat = [piece for pieces in blocks for piece in pieces]
    rows = flat[0].shape[1]
    width = heads * HD
    own = parts * rows
    extra = coarse.shape[1]
    seen = own + extra

    def block_spec(lead, height, total):
        skip = first if total > width else 0
        return pl.BlockSpec((lead, height, HD), lambda h: (0, 0, skip + h))

    outs = pl.pallas_call(
        functools.partial(attention_kernel, layout, depth, pool_size),
        grid=(heads,),
        in_specs=[block_spec(b.shape[0], rows, b.shape[2]) for b in flat]
        + [block_spec(2, extra, coarse.shape[2])],
        out_specs=[block_spec(2, rows, width)] * parts
        + [block_spec(2, own, width), block_spec(2, extra, width)],
        out_shape=[jax.ShapeDtypeStruct((2, rows, width), jnp.bfloat16)] * parts
        + [
            jax.ShapeDtypeStruct((2, own, width), jnp.float32),
            jax.ShapeDtypeStruct((2, extra, width), jnp.float32),
        ],
        compiler_params=pltpu.CompilerParams(vmem_limit_bytes=40 * 1024 * 1024),
        cost_estimate=pl.CostEstimate(
            flops=12 * heads * own * seen * HD,
            bytes_accessed=24 * own * width,
            transcendentals=heads * own * seen,
        ),
        name="attention",
    )(*flat, coarse)
    return outs[:parts], outs[parts], outs[parts + 1]


def held(array):
    hbm = pl.BlockSpec(memory_space=pltpu.HBM)
    return pl.pallas_call(
        lambda *refs: None,
        in_specs=[hbm],
        out_specs=hbm,
        out_shape=jax.ShapeDtypeStruct(array.shape, array.dtype),
        input_output_aliases={0: 0},
        name="held",
    )(array)


def on_device(queries, keys_in, values_in, grad_out):
    seq_count = lax.axis_size("seq")
    parts = lax.axis_size("head")
    me = lax.axis_index("head")
    depth = seq_count.bit_length() - 1
    rows, columns = queries.shape
    own = rows * parts
    pool_size = own // CROWS
    per = rows // pool_size
    width = columns // parts
    heads = width // HD
    split = [heads - heads // 2, heads // 2][: min(heads, 2)]
    groups = len(split)
    starts = [sum(split[:g]) for g in range(groups)]
    far = range(2, parts)
    arrays = (keys_in, values_in, queries, grad_out)

    def column(part, head=0):
        return (me ^ part) * width + head * HD

    def slab(part, head, size):
        return jnp.stack(
            [lax.dynamic_slice_in_dim(x, column(part, head), size, axis=1) for x in arrays]
        )

    landed = {}

    def send(block, part, name):
        landed[name] = swapped(block, "head", part)

    def after(block, names):
        for name in names:
            if name in landed:
                block, landed[name] = lax.optimization_barrier((block, landed[name]))
        return block

    def pieces(part, g):
        whole = slab(part, starts[g], split[g] * HD)
        return [whole[:2], whole[2:]] if g == 0 and part == 2 else [whole]

    both = jnp.concatenate([keys_in, values_in])
    opening = lax.dynamic_slice_in_dim(both, column(2), split[0] * HD, axis=1)
    opening = opening.reshape(2, rows, split[0] * HD)
    keys_in, values_in = lax.optimization_barrier((keys_in, values_in))
    arrays = (keys_in, values_in, queries, grad_out)
    slabs = [[pieces(part, g) for part in far] for g in range(groups)]
    others = (slabs[0][0][1:], slabs[0][1:])
    others, keys_now, values_now = lax.optimization_barrier((others, keys_in, values_in))
    slabs[0] = [[opening, *others[0]], *others[1]]
    pooled_here = jnp.stack(
        [
            jnp.mean(x.astype(jnp.float32).reshape(per, pool_size, columns), axis=1)
            for x in (keys_now, values_now)
        ]
    )
    pooled_parts = []
    for part in range(parts):
        block = lax.dynamic_slice_in_dim(pooled_here, column(part), width, axis=2)
        pooled_parts.append(swapped(block, "head", part) if part else block)
    send(slabs[0][0][0], 2, ("in", 0, 2, 0))
    mean_now = jnp.concatenate(pooled_parts, axis=1)
    for g in range(groups):
        send(slab(1, starts[g], split[g] * HD), 1, ("near", g))
    siblings = []
    for level in range(depth):
        if level < len(PACE_IN):
            mean_now = after(mean_now, PACE_IN[level])
        received = swapped(mean_now, "seq", 1 << level)
        siblings.append(received)
        mean_now = 0.5 * (mean_now + received)

    blocks = []
    for g in range(groups):
        if g:
            at = min(2, depth) - 1
            slabs[g], siblings[at] = lax.optimization_barrier((slabs[g], siblings[at]))
        for part in far:
            for at, piece in enumerate(slabs[g][part - 2]):
                if ("in", g, part, at) not in landed:
                    send(piece, part, ("in", g, part, at))
        blocks.append([[slab(0, starts[g], split[g] * HD)], [landed["near", g]]])
    coarse = jnp.concatenate(siblings, axis=1).astype(jnp.bfloat16)

    kept, grads, sums = [], [], []
    for g in range(groups):
        blocks[g][1] = [landed["near", g]]
        here = blocks[g] + [
            [landed["in", g, part, at] for at in range(len(slabs[g][part - 2]))] for part in far
        ]
        sent, local, coarse_grad = attention(here, coarse, starts[g], split[g], depth, pool_size)
        kept.append(sent)
        grads.append(local)
        sums.append(coarse_grad.reshape(2, depth, CROWS, split[g] * HD))
        for part in far:
            send(sent[part], part, ("mid", g, part))

    def chain(coarse_grad, pace, low):
        pace = list(pace) + [()] * (depth + 1)
        coarse_grad = after(coarse_grad, pace[0])
        above = jnp.zeros(coarse_grad[:, 0].shape, jnp.float32)
        for level in reversed(range(depth)):
            outgoing = coarse_grad[:, level] + 0.5 * above
            if level in low:
                outgoing = outgoing.astype(jnp.bfloat16)
            received = swapped(outgoing, "seq", 1 << level)
            received = after(received, pace[depth - level])
            above = 0.5 * above + received.astype(jnp.float32)
        return above / float(pool_size)

    def total(part, local, above):
        spread = jnp.repeat(above[:, part * per : (part + 1) * per], pool_size, axis=1)
        return (local[:, part * rows : (part + 1) * rows] + spread).astype(jnp.bfloat16)

    own_last, near_last = [], []
    for g in range(groups):
        above = chain(sums[g], PACE[g], LOW[g])
        for part in far:
            block = total(part, grads[g], above)
            if g == groups - 1:
                send(block[:1], part, ("last", g, part, 0))
                send(block[1:], part, ("last", g, part, 1))
            else:
                send(block, part, ("last", g, part))
        own_last.append(total(0, grads[g], above))
        near_last.append(total(1, grads[g], above))
    near = [swapped(kept[g][1], "head", 1) for g in range(groups)]
    near_last = [swapped(block, "head", 1) for block in near_last]

    outs = [jnp.zeros((rows, columns), jnp.bfloat16) for _ in range(4)]

    def place(first, back, part, head=0):
        for which in range(back.shape[0]):
            outs[first + which] = lax.dynamic_update_slice(
                outs[first + which], back[which], (0, column(part, head))
            )

    for g in range(groups):
        place(0, kept[g][0], 0, starts[g])
        place(0, near[g], 1, starts[g])
        place(2, own_last[g], 0, starts[g])
        place(2, near_last[g], 1, starts[g])
        for part in far:
            place(0, landed["mid", g, part], part, starts[g])
            if g < groups - 1:
                place(2, landed["last", g, part], part, starts[g])
            else:
                place(2, landed["last", g, part, 0], part, starts[g])
    for at, part in enumerate(reversed(far)):
        if at == 1:
            outs[3] = held(outs[3])
        place(3, landed["last", groups - 1, part, 1], part, starts[-1])
    return tuple(outs)


def solution(mesh):
    placed = (P(("seq", "head"), None),) * 4
    return jax.shard_map(
        on_device, mesh=mesh, in_specs=placed, out_specs=placed, check_vma=False
    )
```

```python
import functools
import math

import jax
import jax.numpy as jnp
from jax import lax
from jax.experimental import pallas as pl
from jax.experimental.pallas import tpu as pltpu
from jax.sharding import PartitionSpec as P

HD = 128
CROWS = 16
SCALE = HD**-0.5
LOW = ((2,), ())
PACE = (
    (),
    ((("mid", 0, 2),), (("mid", 0, 3),), (("last", 0, 2),), (("last", 0, 3),)),
)
PACE_IN = ((("in", 0, 2, 0),), (), (("near", 1),))


def swapped(block, axis, mask):
    count = lax.axis_size(axis)
    return lax.ppermute(block, axis, [(i, i ^ mask) for i in range(count)])


def attention_kernel(layout, depth, pool_size, *refs):
    parts, count = len(layout), sum(len(sizes) for sizes in layout)
    blocks, at = [], 0
    for sizes in layout:
        blocks.append([(ref, i) for ref, size in zip(refs[at:], sizes) for i in range(size)])
        at += len(sizes)
    coarse_ref = refs[count]
    out_refs = refs[count + 1 : count + 1 + parts]
    local_ref, coarse_grad_ref = refs[count + 1 + parts :]
    rows = refs[0].shape[1]
    own = parts * rows

    def whole(which):
        return jnp.concatenate([block[which][0][block[which][1]] for block in blocks], axis=0)

    keys = jnp.concatenate([whole(0), coarse_ref[0]], axis=0)
    values = jnp.concatenate([whole(1), coarse_ref[1]], axis=0)
    queries, grads = whole(2), whole(3)
    seen = keys.shape[0]

    def dot(a, b, over):
        return lax.dot_general(
            a, b, (((over[0],), (over[1],)), ((), ())), preferred_element_type=jnp.float32
        )

    scores = dot(keys, queries, (1, 1)) * (SCALE * math.log2(math.e))
    row = lax.broadcasted_iota(jnp.int32, (seen - own, 1), 0)
    offset = (row // CROWS).astype(jnp.float32) + math.log2(pool_size)
    scores = jnp.concatenate([scores[:own], scores[own:] + offset], axis=0)
    powers = jnp.exp2(scores - jnp.max(scores, axis=0, keepdims=True))
    probs = powers * (1.0 / jnp.sum(powers, axis=0, keepdims=True))
    probs_low = probs.astype(jnp.bfloat16)
    dprob = dot(values, grads, (1, 1))
    mean = jnp.sum(probs * dprob, axis=0, keepdims=True)
    dscore = (probs * SCALE * (dprob - mean)).astype(jnp.bfloat16)
    attended = dot(values, probs_low, (0, 0)).T.astype(jnp.bfloat16)
    grad_query = dot(keys, dscore, (0, 0)).T.astype(jnp.bfloat16)
    dkeys = dot(dscore, queries, (1, 0))
    dvalues = dot(probs_low, grads, (1, 0))
    for part in range(parts):
        here = slice(part * rows, (part + 1) * rows)
        out_refs[part][0] = attended[here]
        out_refs[part][1] = grad_query[here]
    local_ref[0] = dkeys[:own]
    local_ref[1] = dvalues[:own]
    coarse_grad_ref[0] = dkeys[own:]
    coarse_grad_ref[1] = dvalues[own:]


def attention(blocks, coarse, first, heads, depth, pool_size):
    parts = len(blocks)
    layout = tuple(tuple(piece.shape[0] for piece in pieces) for pieces in blocks)
    flat = [piece for pieces in blocks for piece in pieces]
    rows = flat[0].shape[1]
    width = heads * HD
    own = parts * rows
    extra = coarse.shape[1]
    seen = own + extra

    def block_spec(lead, height, total):
        skip = first if total > width else 0
        return pl.BlockSpec((lead, height, HD), lambda h: (0, 0, skip + h))

    outs = pl.pallas_call(
        functools.partial(attention_kernel, layout, depth, pool_size),
        grid=(heads,),
        in_specs=[block_spec(b.shape[0], rows, b.shape[2]) for b in flat]
        + [block_spec(2, extra, coarse.shape[2])],
        out_specs=[block_spec(2, rows, width)] * parts
        + [block_spec(2, own, width), block_spec(2, extra, width)],
        out_shape=[jax.ShapeDtypeStruct((2, rows, width), jnp.bfloat16)] * parts
        + [
            jax.ShapeDtypeStruct((2, own, width), jnp.float32),
            jax.ShapeDtypeStruct((2, extra, width), jnp.float32),
        ],
        compiler_params=pltpu.CompilerParams(vmem_limit_bytes=40 * 1024 * 1024),
        cost_estimate=pl.CostEstimate(
            flops=12 * heads * own * seen * HD,
            bytes_accessed=24 * own * width,
            transcendentals=heads * own * seen,
        ),
        name="attention",
    )(*flat, coarse)
    return outs[:parts], outs[parts], outs[parts + 1]


def held(array):
    hbm = pl.BlockSpec(memory_space=pltpu.HBM)
    return pl.pallas_call(
        lambda *refs: None,
        in_specs=[hbm],
        out_specs=hbm,
        out_shape=jax.ShapeDtypeStruct(array.shape, array.dtype),
        input_output_aliases={0: 0},
        name="held",
    )(array)


def on_device(queries, keys_in, values_in, grad_out):
    seq_count = lax.axis_size("seq")
    parts = lax.axis_size("head")
    me = lax.axis_index("head")
    depth = seq_count.bit_length() - 1
    rows, columns = queries.shape
    own = rows * parts
    pool_size = own // CROWS
    per = rows // pool_size
    width = columns // parts
    heads = width // HD
    split = [heads - heads // 2, heads // 2][: min(heads, 2)]
    groups = len(split)
    starts = [sum(split[:g]) for g in range(groups)]
    far = range(2, parts)
    arrays = (keys_in, values_in, queries, grad_out)

    def column(part, head=0):
        return (me ^ part) * width + head * HD

    def slab(part, head, size):
        return jnp.stack(
            [lax.dynamic_slice_in_dim(x, column(part, head), size, axis=1) for x in arrays]
        )

    landed = {}

    def send(block, part, name):
        landed[name] = swapped(block, "head", part)

    def after(block, names):
        for name in names:
            if name in landed:
                block, landed[name] = lax.optimization_barrier((block, landed[name]))
        return block

    def pieces(part, g):
        whole = slab(part, starts[g], split[g] * HD)
        return [whole[:2], whole[2:]] if g == 0 and part == 2 else [whole]

    both = jnp.concatenate([keys_in, values_in])
    opening = lax.dynamic_slice_in_dim(both, column(2), split[0] * HD, axis=1)
    opening = opening.reshape(2, rows, split[0] * HD)
    keys_in, values_in = lax.optimization_barrier((keys_in, values_in))
    arrays = (keys_in, values_in, queries, grad_out)
    slabs = [[pieces(part, g) for part in far] for g in range(groups)]
    others = (slabs[0][0][1:], slabs[0][1:])
    others, keys_now, values_now = lax.optimization_barrier((others, keys_in, values_in))
    slabs[0] = [[opening, *others[0]], *others[1]]
    pooled_here = jnp.stack(
        [
            jnp.mean(x.astype(jnp.float32).reshape(per, pool_size, columns), axis=1)
            for x in (keys_now, values_now)
        ]
    )
    pooled_parts = []
    for part in range(parts):
        block = lax.dynamic_slice_in_dim(pooled_here, column(part), width, axis=2)
        pooled_parts.append(swapped(block, "head", part) if part else block)
    send(slabs[0][0][0], 2, ("in", 0, 2, 0))
    mean_now = jnp.concatenate(pooled_parts, axis=1)
    for g in range(groups):
        send(slab(1, starts[g], split[g] * HD), 1, ("near", g))
    siblings = []
    for level in range(depth):
        if level < len(PACE_IN):
            mean_now = after(mean_now, PACE_IN[level])
        received = swapped(mean_now, "seq", 1 << level)
        siblings.append(received)
        mean_now = 0.5 * (mean_now + received)

    blocks = []
    for g in range(groups):
        if g:
            at = min(2, depth) - 1
            slabs[g], siblings[at] = lax.optimization_barrier((slabs[g], siblings[at]))
        for part in far:
            for at, piece in enumerate(slabs[g][part - 2]):
                if ("in", g, part, at) not in landed:
                    send(piece, part, ("in", g, part, at))
        blocks.append([[slab(0, starts[g], split[g] * HD)], [landed["near", g]]])
    coarse = jnp.concatenate(siblings, axis=1).astype(jnp.bfloat16)

    kept, grads, sums = [], [], []
    for g in range(groups):
        blocks[g][1] = [landed["near", g]]
        here = blocks[g] + [
            [landed["in", g, part, at] for at in range(len(slabs[g][part - 2]))] for part in far
        ]
        sent, local, coarse_grad = attention(here, coarse, starts[g], split[g], depth, pool_size)
        kept.append(sent)
        grads.append(local)
        sums.append(coarse_grad.reshape(2, depth, CROWS, split[g] * HD))
        for part in far:
            send(sent[part], part, ("mid", g, part))

    def chain(coarse_grad, pace, low):
        pace = list(pace) + [()] * (depth + 1)
        coarse_grad = after(coarse_grad, pace[0])
        above = jnp.zeros(coarse_grad[:, 0].shape, jnp.float32)
        for level in reversed(range(depth)):
            outgoing = coarse_grad[:, level] + 0.5 * above
            if level in low:
                outgoing = outgoing.astype(jnp.bfloat16)
            received = swapped(outgoing, "seq", 1 << level)
            received = after(received, pace[depth - level])
            above = 0.5 * above + received.astype(jnp.float32)
        return above / float(pool_size)

    def total(part, local, above):
        spread = jnp.repeat(above[:, part * per : (part + 1) * per], pool_size, axis=1)
        return (local[:, part * rows : (part + 1) * rows] + spread).astype(jnp.bfloat16)

    own_last, near_last = [], []
    for g in range(groups):
        above = chain(sums[g], PACE[g], LOW[g])
        for part in far:
            block = total(part, grads[g], above)
            if g == groups - 1:
                send(block[:1], part, ("last", g, part, 0))
                send(block[1:], part, ("last", g, part, 1))
            else:
                send(block, part, ("last", g, part))
        own_last.append(total(0, grads[g], above))
        near_last.append(total(1, grads[g], above))
    near = [swapped(kept[g][1], "head", 1) for g in range(groups)]
    near_last = [swapped(block, "head", 1) for block in near_last]

    outs = [jnp.zeros((rows, columns), jnp.bfloat16) for _ in range(4)]

    def place(first, back, part, head=0):
        for which in range(back.shape[0]):
            outs[first + which] = lax.dynamic_update_slice(
                outs[first + which], back[which], (0, column(part, head))
            )

    for g in range(groups):
        place(0, kept[g][0], 0, starts[g])
        place(0, near[g], 1, starts[g])
        place(2, own_last[g], 0, starts[g])
        place(2, near_last[g], 1, starts[g])
        for part in far:
            place(0, landed["mid", g, part], part, starts[g])
            if g < groups - 1:
                place(2, landed["last", g, part], part, starts[g])
            else:
                place(3, landed["last", g, part, 1], part, starts[g])
    for at, part in enumerate(far):
        if at == 1:
            outs[2] = held(outs[2])
        place(2, landed["last", groups - 1, part, 0], part, starts[-1])
    return tuple(outs)


def solution(mesh):
    placed = (P(("seq", "head"), None),) * 4
    return jax.shard_map(
        on_device, mesh=mesh, in_specs=placed, out_specs=placed, check_vma=False
    )
```
